32 devices in a mesh: grp: 2 (over x), tile: 16 (over z, y, core).
Axes of the slice: x: 2, y: 2, z: 4, core: 2. Of those that a mesh axis runs over, the one named last changes fastest.
Arguments:
- mask_params: float32 [64, 64, 128], P(('grp', 'tile')), parts along dimension 0, may hold values from -3 to 3
- target: float32 [64, 64, 128], P(('grp', 'tile')), parts along dimension 0, may hold values from 0 to 1
- weight: float32 [64, 64, 128], P(('grp', 'tile')), parts along dimension 0, may hold values from 0.3 to 3
- kernels: float32 [24, 2, 65, 65], replicated, may hold values from -0.25515518 to 0.25515518
- kernel_weight: float32 [24], replicated, may hold values from 0.05 to 1
- tile_ids: int32 [64], P(('grp', 'tile')), parts along dimension 0, may hold values from -1 to 134, as said below
- tile_links: int32 [64, 2], P(('grp', 'tile')), parts along dimension 0, may hold values from 0 to 1, as said below
Outputs:
- params_out: float32 [64, 64, 128], P(('grp', 'tile')), parts along dimension 0
- resist: float32 [64, 64, 128], P(('grp', 'tile')), parts along dimension 0
The draws below stay inside these ranges and needn't reach their ends.
There are 2 independent parts, one for each index of `grp`. The reference program is written for one: setup_inputs(seed, part) draws one part's arguments, and reference() takes and returns one part's arrays. A program takes and returns all parts, laid end to end along the dimension named above; an argument that names none is the same for every part. Nothing has to cross between parts.
Inputs may be any that keep to these rules, and one draw needn't show every extreme that they name: `tile_ids`: -1 marks an empty slot. Every device holds between 1 and 2 tiles in its first slots and some device holds 2; stripe columns rise strictly in the order of devices and slots, and the last live tile of the stripe holds column 134. `tile_links`: entry 0 is 1 exactly where the stripe column just before the slot's tile holds an active tile (then held by the previous live slot in order), entry 1 likewise for the column just after (the next live slot); both are 0 for empty slots.
All inputs are finite; a program needn't handle non-finite values.
Results may differ from the reference program's by a relative error of at most 0.00011.
Values sent between devices are 32-bit elements; how exact they have to be, the bound alone decides.
A program may use at most 64 MiB of HBM per device.

```python
import math
import jax
import jax.numpy as jnp
from jax import lax

SX = 128
SY = 64
TD = 2
K = 24
FREQ = 65
ITERS = 2
TILES = 32


def layout_draw(key):
    base = jax.random.fold_in(key, 4111)
    key_list = jax.random.split(base, 6)
    device_total = TILES // TD
    busy_device = jax.random.randint(key_list[0], (device_total,), 0, 4) == 0
    extra_tiles = jax.random.randint(key_list[1], (device_total,), 0, max(TD - 1, 1))
    filled = jnp.where(busy_device, TD, 1 + extra_tiles)
    chosen = jax.random.randint(key_list[2], (), 0, device_total)
    filled = jnp.where(jnp.arange(device_total) == chosen, TD, filled)
    slot_index = jnp.arange(TD)
    active = (slot_index[None, :] < filled[:, None]).reshape(-1)
    skip_pick = jax.random.randint(key_list[3], (TILES,), 0, 4) == 0
    skip_size = jax.random.randint(key_list[4], (TILES,), 1, 4)
    skipped = jnp.where(skip_pick, skip_size, 0)
    start_col = jax.random.randint(key_list[5], (), 0, 8)
    advance = jnp.where(active, 1 + skipped, 0).astype(jnp.int32)
    column = jnp.cumsum(advance).astype(jnp.int32) - 1 + start_col
    last_column = jnp.max(jnp.where(active, column, -1)).astype(jnp.int32)
    shifted = column - last_column + (4 * TILES + 6)
    tile_ids = jnp.where(active, shifted, -1).astype(jnp.int32)
    position = jnp.arange(TILES, dtype=jnp.int32)
    left_link = (active & (skipped == 0) & (position > 0)).astype(jnp.int32)
    ahead_slot = lax.cummin(jnp.where(active, position, TILES), reverse=True)
    next_slot = jnp.concatenate([ahead_slot[1:].astype(jnp.int32), jnp.full((1,), TILES, jnp.int32)])
    has_next = active & (next_slot < TILES)
    right_link = jnp.where(has_next, left_link[jnp.clip(next_slot, 0, TILES - 1)], 0).astype(jnp.int32)
    return (tile_ids, jnp.stack([left_link, right_link], axis=1))


def draw_tile_ids(key, part):
    return layout_draw(key)[0]


def draw_tile_links(key, part):
    return layout_draw(key)[1]


def feature_layout(key):
    rows = jnp.arange(SY, dtype=jnp.int32)[None, :, None]
    cols = jnp.arange(SX, dtype=jnp.int32)[None, None, :]
    feature = jnp.zeros((TILES, SY, SX), dtype=bool)
    for rect in range(5):
        rect_keys = jax.random.split(jax.random.fold_in(key, 7919 + rect), 5)
        top = jax.random.randint(rect_keys[0], (TILES, 1, 1), 0, SY)
        height = jax.random.randint(rect_keys[1], (TILES, 1, 1), max(SY // 8, 1), SY // 2 + 1)
        left = jax.random.randint(rect_keys[2], (TILES, 1, 1), 0, SX)
        breadth = jax.random.randint(rect_keys[3], (TILES, 1, 1), max(SX // 4, 1), SX + 1)
        kept = jax.random.randint(rect_keys[4], (TILES, 1, 1), 0, 5) < 3
        inside = kept & (rows >= top) & (rows < top + height) & (cols >= left) & (cols < left + breadth)
        feature = feature | inside
    return jnp.where(feature, 1.0, -1.0).astype(jnp.float32)


def draw_mask_params(key, part):
    signs = feature_layout(jax.random.fold_in(key, 3301))
    noise_key = jax.random.fold_in(key, 3313)
    amplitude = 1.5
    noise = 0.6 * jax.random.normal(noise_key, (TILES, SY, SX), jnp.float32)
    return jnp.clip(amplitude * signs + noise, -3.0, 3.0).astype(jnp.float32)


def draw_kernels(key, part):
    spread = 0.35 / math.sqrt(K)
    bound = 1.25 / math.sqrt(K)
    shape = (K, 2, FREQ, FREQ)
    base_key = jax.random.fold_in(key, 5501)
    values = spread * jax.random.normal(base_key, shape, jnp.float32)
    return jnp.clip(values, -bound, bound).astype(jnp.float32)


def shard_levels(stream_key, dims, cuts, least, largest):
    loudness, own = 1.0, jax.random.fold_in(stream_key, 6)
    for dim, parts in cuts:
        draws = jnp.exp(jax.random.uniform(jax.random.fold_in(own, dim), (parts,), jnp.float32, least / len(cuts), largest / len(cuts)))
        loudness = loudness * jnp.repeat(draws, dims[dim] // parts).reshape([-1 if axis == dim else 1 for axis in range(len(dims))])
    return loudness


def setup_inputs(seed: int = 0, part: int = 0) -> dict:
    key_of = jax.random.split(jax.random.key(seed), 8)
    part_keys = jax.random.split(jax.random.fold_in(key_of[7], part), 8)
    mask_params = draw_mask_params(jax.random.fold_in(jax.random.fold_in(key_of[7], part), 71), part)
    target = jnp.clip(1.0 * jax.random.uniform(part_keys[1], (TILES, SY, SX), jnp.float32) ** shard_levels(part_keys[1], (TILES, SY, SX), ((0, 16),), -0.2, 0.2), 0.0, 1.0)
    weight = jnp.clip(jnp.exp(math.log(3.0) - 2.3025851 * jax.random.uniform(part_keys[2], (TILES, SY, SX), jnp.float32) ** shard_levels(part_keys[2], (TILES, SY, SX), ((0, 16),), -0.2, 0.2)), 0.3, 3.0)
    kernels = draw_kernels(jax.random.fold_in(key_of[7], 71), part)
    kernel_weight = jnp.clip(jnp.exp(jax.random.uniform(key_of[4], (K,), jnp.float32, math.log(0.05), math.log(1.0))), 0.05, 1.0)
    tile_ids = draw_tile_ids(jax.random.fold_in(jax.random.fold_in(key_of[7], part), 71), part)
    tile_links = draw_tile_links(jax.random.fold_in(jax.random.fold_in(key_of[7], part), 71), part)
    return {"mask_params": mask_params, "target": target, "weight": weight, "kernels": kernels, "kernel_weight": kernel_weight, "tile_ids": tile_ids, "tile_links": tile_links}


HIGHEST = lax.Precision.HIGHEST
RESIST_SLOPE = 4.0
THRESHOLD = 0.9
STEP_SCALE = 0.04

def phase_table(length, period, band_count, offset):
    half_band = (band_count - 1) // 2
    positions = jnp.arange(length, dtype=jnp.int32) + offset
    frequency = jnp.arange(band_count, dtype=jnp.int32) - half_band
    turn_count = positions[:, None] * frequency[None, :] % period
    angles = turn_count.astype(jnp.float32) * (2.0 * math.pi / period)
    return (jnp.cos(angles), jnp.sin(angles))

def matmul_high(matrix_a, matrix_b):
    return jnp.dot(matrix_a, matrix_b, precision=HIGHEST)

def einsum_high(pattern, first_op, second_op):
    return jnp.einsum(pattern, first_op, second_op, precision=HIGHEST)

def spectral_core(spec_real, spec_imag, target_tile, weight_tile, kernel_real, kernel_imag, kernel_weight, row_cos, row_sin, own_cos, own_sin):
    drive_real = kernel_real * spec_real - kernel_imag * spec_imag
    drive_imag = kernel_real * spec_imag + kernel_imag * spec_real
    rows_real = einsum_high('yf,kfg->kgy', row_cos, drive_real) - einsum_high('yf,kfg->kgy', row_sin, drive_imag)
    rows_imag = einsum_high('yf,kfg->kgy', row_cos, drive_imag) + einsum_high('yf,kfg->kgy', row_sin, drive_real)
    field_real = einsum_high('kgy,xg->kyx', rows_real, own_cos) - einsum_high('kgy,xg->kyx', rows_imag, own_sin)
    field_imag = einsum_high('kgy,xg->kyx', rows_real, own_sin) + einsum_high('kgy,xg->kyx', rows_imag, own_cos)
    intensity = einsum_high('k,kyx->yx', kernel_weight, field_real * field_real + field_imag * field_imag)
    resist_now = jax.nn.sigmoid(RESIST_SLOPE * (intensity - THRESHOLD))
    slope_map = 2.0 * weight_tile * (resist_now - target_tile) * RESIST_SLOPE * resist_now * (1.0 - resist_now)
    back_real = slope_map * field_real
    back_imag = -slope_map * field_imag
    cols_real = einsum_high('kyx,xg->kgy', back_real, own_cos) - einsum_high('kyx,xg->kgy', back_imag, own_sin)
    cols_imag = einsum_high('kyx,xg->kgy', back_real, own_sin) + einsum_high('kyx,xg->kgy', back_imag, own_cos)
    freq_real = einsum_high('yf,kgy->kfg', row_cos, cols_real) - einsum_high('yf,kgy->kfg', row_sin, cols_imag)
    freq_imag = einsum_high('yf,kgy->kfg', row_cos, cols_imag) + einsum_high('yf,kgy->kfg', row_sin, cols_real)
    sum_real = einsum_high('k,kfg->fg', kernel_weight, kernel_real * freq_real - kernel_imag * freq_imag)
    sum_imag = einsum_high('k,kfg->fg', kernel_weight, kernel_real * freq_imag + kernel_imag * freq_real)
    return (resist_now, sum_real, sum_imag)

def tile_spectrum(pixels, row_cos, row_sin, col_cos, col_sin, unit_area):
    part_real = matmul_high(pixels, col_cos)
    part_imag = -matmul_high(pixels, col_sin)
    spec_real = (matmul_high(row_cos.T, part_real) + matmul_high(row_sin.T, part_imag)) * unit_area
    spec_imag = (matmul_high(row_cos.T, part_imag) - matmul_high(row_sin.T, part_real)) * unit_area
    return (spec_real, spec_imag)

def back_to_pixels(sum_real, sum_imag, row_cos, row_sin, col_cos, col_sin, unit_area):
    upper_real = matmul_high(row_cos, sum_real) + matmul_high(row_sin, sum_imag)
    upper_imag = matmul_high(row_cos, sum_imag) - matmul_high(row_sin, sum_real)
    return (matmul_high(upper_real, col_cos.T) + matmul_high(upper_imag, col_sin.T)) * (2.0 * unit_area)

def reference(mask_params, target, weight, kernels, kernel_weight, tile_ids, tile_links):
    slot_total, tile_rows, tile_cols = mask_params.shape
    band_count = kernels.shape[2]
    unit_area = 1.0 / (tile_rows * tile_cols)
    step_size = STEP_SCALE * math.sqrt(tile_rows * tile_cols)
    row_cos, row_sin = phase_table(tile_rows, 2 * tile_rows, band_count, 0)
    domain_cos, domain_sin = phase_table(3 * tile_cols, 3 * tile_cols, band_count, 0)
    own_cos = domain_cos[tile_cols:2 * tile_cols]
    own_sin = domain_sin[tile_cols:2 * tile_cols]
    kernel_real = kernels[:, 0]
    kernel_imag = kernels[:, 1]
    active = tile_ids >= 0
    slot_index = jnp.arange(slot_total, dtype=jnp.int32)
    seen_live = lax.cummax(jnp.where(active, slot_index, -1))
    before_slot = jnp.concatenate([jnp.full((1,), -1, jnp.int32), seen_live[:-1].astype(jnp.int32)])
    ahead_slot = lax.cummin(jnp.where(active, slot_index, slot_total), reverse=True)
    after_slot = jnp.concatenate([ahead_slot[1:].astype(jnp.int32), jnp.full((1,), slot_total, jnp.int32)])
    before_slot = jnp.clip(before_slot, 0, slot_total - 1)
    after_slot = jnp.clip(after_slot, 0, slot_total - 1)
    left_on = (tile_links[:, 0] == 1)[:, None, None]
    right_on = (tile_links[:, 1] == 1)[:, None, None]
    active_grid = active[:, None, None]

    def domain_pass(pieces):
        domain, target_tile, weight_tile = pieces
        spec_real, spec_imag = tile_spectrum(domain, row_cos, row_sin, domain_cos, domain_sin, unit_area)
        resist_now, sum_real, sum_imag = spectral_core(spec_real, spec_imag, target_tile, weight_tile, kernel_real, kernel_imag, kernel_weight, row_cos, row_sin, own_cos, own_sin)
        return (resist_now, back_to_pixels(sum_real, sum_imag, row_cos, row_sin, domain_cos, domain_sin, unit_area))
    resist_now = jnp.zeros_like(mask_params)
    for sweep in range(ITERS):
        transmit = jnp.tanh(mask_params)
        left_tiles = jnp.where(left_on, transmit[before_slot], 0.0)
        right_tiles = jnp.where(right_on, transmit[after_slot], 0.0)
        domain = jnp.concatenate([left_tiles, transmit, right_tiles], axis=2)
        resist_now, domain_grads = lax.map(domain_pass, (domain, target, weight))
        gradient = domain_grads[:, :, tile_cols:2 * tile_cols]
        gradient = gradient + jnp.where(left_on, domain_grads[before_slot][:, :, 2 * tile_cols:], 0.0)
        gradient = gradient + jnp.where(right_on, domain_grads[after_slot][:, :, :tile_cols], 0.0)
        mask_params = jnp.where(active_grid, mask_params - step_size * gradient * (1.0 - transmit * transmit), mask_params)
    resist_out = jnp.where(active_grid, resist_now, 0.0)
    return (mask_params, resist_out)
```

```python
import functools
import math

import jax
import jax.numpy as jnp
import ml_dtypes
import numpy as np
from jax import lax
from jax.experimental import pallas as pl
from jax.experimental.pallas import tpu as pltpu
from jax.sharding import PartitionSpec as P

ITERS = 2
RESIST_SLOPE = 4.0
THRESHOLD = 0.9
STEP_SCALE = 0.04
F32 = jnp.float32
BF16 = jnp.bfloat16


def round_up(size, step):
    return (size + step - 1) // step * step


def phases(length, period, bands):
    f = np.arange(bands, dtype=np.int64) - (bands - 1) // 2
    turns = (np.arange(length, dtype=np.int64)[:, None] * f[None, :]) % period
    angles = turns.astype(np.float64) * (2.0 * math.pi / period)
    return np.cos(angles), np.sin(angles)


def padded(table, rows, cols):
    return np.pad(table, ((0, rows - table.shape[0]), (0, cols - table.shape[1])))


def halves(table):
    table = table.astype(np.float32)
    hi = table.astype(ml_dtypes.bfloat16)
    lo = (table - hi.astype(np.float32)).astype(ml_dtypes.bfloat16)
    return hi, lo


def left_table(table):
    hi, lo = halves(table)
    return np.concatenate([hi, hi, lo], axis=1)


def right_table(table):
    hi, lo = halves(table)
    return np.concatenate([hi, lo, hi], axis=0)


def make_tables(rows, cols, bands):
    fp, fl = round_up(bands, 16), round_up(bands, 128)
    row_cos, row_sin = phases(rows, 2 * rows, bands)
    dom_cos, dom_sin = phases(3 * cols, 3 * cols, bands)
    own = slice(cols, 2 * cols)
    to_rows = np.concatenate([padded(row_cos, rows, fp), padded(row_sin, rows, fp)], axis=1)
    to_freqs = np.concatenate(
        [padded(row_cos.T, fp, rows), padded(row_sin.T, fp, rows)], axis=1
    )
    oc, os = padded(dom_cos[own].T, fl, cols), padded(dom_sin[own].T, fl, cols)
    field = np.block([[oc, os], [-os, oc]])
    adjoint = np.block([[oc.T, os.T], [os.T, -oc.T]])
    dc, ds = padded(dom_cos, 3 * cols, fl), padded(dom_sin, 3 * cols, fl)
    spectrum = np.concatenate([dc, -ds], axis=1)
    gradient = np.concatenate([dc.T, ds.T], axis=0)
    return (
        left_table(to_rows),
        left_table(to_freqs),
        right_table(spectrum),
        right_table(field),
        right_table(adjoint),
        right_table(gradient),
    )


def split(x):
    hi = x.astype(BF16)
    lo = (x - hi.astype(F32)).astype(BF16)
    return hi, lo


def dot(a, b):
    return jnp.dot(a, b, preferred_element_type=F32)


def stream(x, table_ref):
    hi, lo = split(x)
    return dot(jnp.concatenate([hi, hi, lo], axis=1), table_ref[...])


def table_dot(table_ref, x):
    hi, lo = split(x)
    return dot(table_ref[...], jnp.concatenate([hi, lo, hi], axis=0))


def kernel(
    axis,
    n,
    chunk,
    params_ref,
    target_ref,
    weight_ref,
    kernels_ref,
    scale_ref,
    ids_ref,
    links_ref,
    rows_ref,
    freqs_ref,
    spectrum_ref,
    field_ref,
    adjoint_ref,
    gradient_ref,
    out_ref,
    resist_ref,
    h_ref,
    e_ref,
    t_ref,
    send_ref,
    recv_ref,
    send_sems,
    recv_sems,
):
    me = lax.axis_index(axis)
    slots, rows, cols = params_ref.shape
    count, _, bands, _ = kernels_ref.shape
    fp, fl = h_ref.shape[1], h_ref.shape[2] // 2
    unit = 1.0 / (rows * cols)
    step_size = STEP_SCALE * math.sqrt(rows * cols)
    has_left, has_right = me > 0, me < n - 1

    barrier = pltpu.get_barrier_semaphore()

    @pl.when(has_left)
    def _():
        pl.semaphore_signal(
            barrier, inc=1, device_id={axis: me - 1}, device_id_type=pl.DeviceIdType.MESH
        )

    @pl.when(has_right)
    def _():
        pl.semaphore_signal(
            barrier, inc=1, device_id={axis: me + 1}, device_id_type=pl.DeviceIdType.MESH
        )

    peers = jnp.where(has_left, 1, 0) + jnp.where(has_right, 1, 0)
    pl.semaphore_wait(barrier, peers)

    @pl.when(jnp.logical_not(has_left))
    def _():
        for e in range(2 * ITERS):
            recv_ref[e, 0] = jnp.zeros((rows, cols), F32)

    @pl.when(jnp.logical_not(has_right))
    def _():
        for e in range(2 * ITERS):
            recv_ref[e, 1] = jnp.zeros((rows, cols), F32)

    def move(e, side):
        return pltpu.make_async_remote_copy(
            src_ref=send_ref.at[e, side],
            dst_ref=recv_ref.at[e, side],
            send_sem=send_sems.at[e, side],
            recv_sem=recv_sems.at[e, side],
            device_id={axis: me + 1 if side == 0 else me - 1},
            device_id_type=pl.DeviceIdType.MESH,
        )

    def start(e):
        @pl.when(has_right)
        def _():
            move(e, 0).start()

        @pl.when(has_left)
        def _():
            move(e, 1).start()

    def arrive(e):
        @pl.when(has_left)
        def _():
            move(e, 0).wait_recv()

        @pl.when(has_right)
        def _():
            move(e, 1).wait_recv()

    live = [ids_ref[s] >= 0 for s in range(slots)]
    left_on = [jnp.where(links_ref[s, 0] == 1, 1.0, 0.0) for s in range(slots)]
    right_on = [jnp.where(links_ref[s, 1] == 1, 1.0, 0.0) for s in range(slots)]

    def last_live(values):
        last = values[0]
        for s in range(1, slots):
            last = jnp.where(live[s], values[s], last)
        return last

    def neighbours(to_right, to_left, e):
        befores, afters = [], []
        for s in range(slots):
            before = recv_ref[e, 0] if s == 0 else to_right[s - 1]
            after = recv_ref[e, 1]
            if s + 1 < slots:
                after = jnp.where(live[s + 1], to_left[s + 1], after)
            befores.append(before * left_on[s])
            afters.append(after * right_on[s])
        return befores, afters

    for it in range(ITERS):
        source = params_ref if it == 0 else out_ref
        transmit = [jnp.tanh(source[s]) for s in range(slots)]
        for s in range(slots):
            t_ref[s] = transmit[s]
        send_ref[2 * it, 0] = last_live(transmit)
        send_ref[2 * it, 1] = transmit[0]
        start(2 * it)

        if it == 0:

            def prepare(k, carry):
                scale = jnp.sqrt(jnp.full((bands, bands), scale_ref[k], F32))
                h_ref[k] = jnp.zeros((fp, 2 * fl), F32)
                h_ref[k, :bands, :bands] = kernels_ref[k, 0] * scale
                h_ref[k, :bands, fl : fl + bands] = kernels_ref[k, 1] * scale
                return carry

            lax.fori_loop(0, count, prepare, 0)

        arrive(2 * it)
        transmit = [t_ref[s] for s in range(slots)]
        befores, afters = neighbours(transmit, transmit, 2 * it)
        domain = jnp.concatenate(
            [
                jnp.concatenate([befores[s], transmit[s], afters[s]], axis=1)
                for s in range(slots)
            ],
            axis=0,
        )
        parts = stream(domain, spectrum_ref)
        spectra = []
        for s in range(slots):
            pr = parts[s * rows : (s + 1) * rows, :fl]
            pi = parts[s * rows : (s + 1) * rows, fl:]
            top = jnp.concatenate([pr, pi], axis=1)
            low = jnp.concatenate([pi, -pr], axis=1)
            spectra.append(table_dot(freqs_ref, jnp.concatenate([top, low], axis=0)) * unit)

        def forward(c, intensities):
            out = []
            for s in range(slots):
                cr, ci = spectra[s][:, :fl], spectra[s][:, fl:]
                mids = []
                for j in range(chunk):
                    k = c * chunk + j
                    hr, hi = h_ref[k, :, :fl], h_ref[k, :, fl:]
                    dr = hr * cr - hi * ci
                    di = hr * ci + hi * cr
                    top = jnp.concatenate([dr, di], axis=1)
                    low = jnp.concatenate([-di, dr], axis=1)
                    mids.append(table_dot(rows_ref, jnp.concatenate([top, low], axis=0)))
                fields = stream(jnp.concatenate(mids, axis=0), field_ref)
                e_ref[s, c] = fields
                total = intensities[s]
                for j in range(chunk):
                    er = fields[j * rows : (j + 1) * rows, :cols]
                    ei = fields[j * rows : (j + 1) * rows, cols:]
                    total = total + er * er + ei * ei
                out.append(total)
            return tuple(out)

        zero = jnp.zeros((rows, cols), F32)
        intensities = lax.fori_loop(0, count // chunk, forward, (zero,) * slots)

        slopes = []
        for s in range(slots):
            now = jax.nn.sigmoid(RESIST_SLOPE * (intensities[s] - THRESHOLD))
            if it == ITERS - 1:
                resist_ref[s] = jnp.where(live[s], now, 0.0)
            slope = 2.0 * weight_ref[s] * (now - target_ref[s]) * RESIST_SLOPE * now * (1.0 - now)
            slopes.append(jnp.concatenate([slope, slope], axis=1))

        def backward(c, sums):
            out = []
            for s in range(slots):
                fields = e_ref[s, c]
                back = jnp.concatenate(
                    [fields[j * rows : (j + 1) * rows] * slopes[s] for j in range(chunk)], axis=0
                )
                columns = stream(back, adjoint_ref)
                sr, si = sums[s]
                for j in range(chunk):
                    k = c * chunk + j
                    gr = columns[j * rows : (j + 1) * rows, :fl]
                    gi = columns[j * rows : (j + 1) * rows, fl:]
                    top = jnp.concatenate([gr, gi], axis=1)
                    low = jnp.concatenate([-gi, gr], axis=1)
                    freq = table_dot(freqs_ref, jnp.concatenate([top, low], axis=0))
                    fr, fi = freq[:, :fl], freq[:, fl:]
                    hr, hi = h_ref[k, :, :fl], h_ref[k, :, fl:]
                    sr = sr + hr * fr - hi * fi
                    si = si + hr * fi + hi * fr
                out.append((sr, si))
            return tuple(out)

        none = jnp.zeros((fp, fl), F32)
        sums = lax.fori_loop(0, count // chunk, backward, ((none, none),) * slots)

        uppers = []
        for s in range(slots):
            sr, si = sums[s]
            top = jnp.concatenate([sr, si], axis=1)
            low = jnp.concatenate([si, -sr], axis=1)
            uppers.append(table_dot(rows_ref, jnp.concatenate([top, low], axis=0)))
        grads = stream(jnp.concatenate(uppers, axis=0), gradient_ref) * (2.0 * unit)
        to_left = [grads[s * rows : (s + 1) * rows, :cols] for s in range(slots)]
        middle = [grads[s * rows : (s + 1) * rows, cols : 2 * cols] for s in range(slots)]
        to_right = [grads[s * rows : (s + 1) * rows, 2 * cols :] for s in range(slots)]
        send_ref[2 * it + 1, 0] = last_live(to_right)
        send_ref[2 * it + 1, 1] = to_left[0]
        start(2 * it + 1)
        arrive(2 * it + 1)
        befores, afters = neighbours(to_right, to_left, 2 * it + 1)
        for s in range(slots):
            gradient = middle[s] + befores[s] + afters[s]
            old = source[s]
            t = t_ref[s]
            new = old - step_size * gradient * (1.0 - t * t)
            out_ref[s] = jnp.where(live[s], new, old)

    for e in range(2 * ITERS):

        @pl.when(has_right)
        def _():
            move(e, 0).wait_send()

        @pl.when(has_left)
        def _():
            move(e, 1).wait_send()


def local(n, mask_params, target, weight, kernels, kernel_weight, tile_ids, tile_links):
    slots, rows, cols = mask_params.shape
    count, _, bands, _ = kernels.shape
    fp, fl = round_up(bands, 16), round_up(bands, 128)
    chunk = next(c for c in (4, 3, 2, 1) if count % c == 0)
    tables = make_tables(rows, cols, bands)
    vmem = pl.BlockSpec(memory_space=pltpu.VMEM)
    smem = pl.BlockSpec(memory_space=pltpu.SMEM)
    shape = jax.ShapeDtypeStruct((slots, rows, cols), F32)
    return pl.pallas_call(
        functools.partial(kernel, "tile", n, chunk),
        out_shape=(shape, shape),
        in_specs=[vmem] * 4 + [smem] * 3 + [vmem] * len(tables),
        out_specs=(vmem, vmem),
        scratch_shapes=[
            pltpu.VMEM((count, fp, 2 * fl), F32),
            pltpu.VMEM((slots, count // chunk, chunk * rows, 2 * cols), F32),
            pltpu.VMEM((slots, rows, cols), F32),
            pltpu.VMEM((2 * ITERS, 2, rows, cols), F32),
            pltpu.VMEM((2 * ITERS, 2, rows, cols), F32),
            pltpu.SemaphoreType.DMA((2 * ITERS, 2)),
            pltpu.SemaphoreType.DMA((2 * ITERS, 2)),
        ],
        compiler_params=pltpu.CompilerParams(
            collective_id=0, has_side_effects=True, vmem_limit_bytes=48 * 1024 * 1024
        ),
    )(
        mask_params,
        target,
        weight,
        kernels,
        kernel_weight,
        tile_ids,
        tile_links,
        *[jnp.asarray(t) for t in tables],
    )


def solution(mesh):
    both = ("grp", "tile")
    return jax.shard_map(
        functools.partial(local, mesh.shape["tile"]),
        mesh=mesh,
        in_specs=(P(both, None, None),) * 3 + (P(), P(), P(both), P(both, None)),
        out_specs=(P(both, None, None),) * 2,
        check_vma=False,
    )
```

```python
import functools
import math

import jax
import jax.numpy as jnp
import ml_dtypes
import numpy as np
from jax import lax
from jax.experimental import pallas as pl
from jax.experimental.pallas import tpu as pltpu
from jax.sharding import PartitionSpec as P

ITERS = 2
RESIST_SLOPE = 4.0
THRESHOLD = 0.9
STEP_SCALE = 0.04
F32 = jnp.float32
BF16 = jnp.bfloat16


def round_up(size, step):
    return (size + step - 1) // step * step


def phases(length, period, bands):
    f = np.arange(bands, dtype=np.int64) - (bands - 1) // 2
    turns = (np.arange(length, dtype=np.int64)[:, None] * f[None, :]) % period
    angles = turns.astype(np.float64) * (2.0 * math.pi / period)
    return np.cos(angles), np.sin(angles)


def padded(table, rows, cols):
    return np.pad(table, ((0, rows - table.shape[0]), (0, cols - table.shape[1])))


def halves(table):
    table = table.astype(np.float32)
    hi = table.astype(ml_dtypes.bfloat16)
    lo = (table - hi.astype(np.float32)).astype(ml_dtypes.bfloat16)
    return hi, lo


def left_table(table):
    hi, lo = halves(table)
    return np.concatenate([hi, hi, lo], axis=1)


def right_table(table):
    hi, lo = halves(table)
    return np.concatenate([hi, lo, hi], axis=0)


def make_tables(rows, cols, bands):
    mid = (bands - 1) // 2
    hp, fl = round_up(mid + 1, 8), round_up(bands, 128)
    row_cos, row_sin = phases(rows, 2 * rows, bands)
    dom_cos, dom_sin = phases(3 * cols, 3 * cols, bands)
    own = slice(cols, 2 * cols)
    sides = np.r_[0:cols, 2 * cols : 3 * cols]
    up_cos, up_sin = padded(row_cos[:, mid:], rows, hp), padded(row_sin[:, mid:], rows, hp)
    to_rows = np.concatenate([up_cos, up_sin], axis=1)
    oc, os = padded(dom_cos[own].T, fl, cols), padded(dom_sin[own].T, fl, cols)
    field = np.block([[oc, os], [-os, oc]])
    adjoint = np.block([[oc.T, os.T], [os.T, -oc.T]])
    dc, ds = padded(dom_cos, 3 * cols, fl), padded(dom_sin, 3 * cols, fl)
    spectrum = np.concatenate([dc, -ds], axis=1)
    gradient = np.concatenate([dc.T, ds.T], axis=0)
    return (
        left_table(to_rows),
        left_table(to_rows.T),
        right_table(spectrum[own]),
        right_table(spectrum[sides]),
        right_table(field),
        right_table(adjoint),
        right_table(gradient[:, own]),
        right_table(gradient[:, sides]),
        fold_table(bands),
    )


def group_of(bands):
    return 8 // math.gcd(2 * bands, 8)


def window_of(bands, j):
    size = round_up(2 * bands + 6, 16)
    begin = min(j * 2 * bands // 8 * 8, group_of(bands) * 2 * bands - size)
    return begin, size


def fold_table(bands):
    mid = (bands - 1) // 2
    hp = round_up(mid + 1, 8)
    tables = []
    for j in range(group_of(bands)):
        begin, size = window_of(bands, j)
        table = np.zeros((4 * hp, size), np.float32)
        first = j * 2 * bands - begin
        for part in range(2):
            for i in range(mid + 1):
                table[2 * part * hp + i, first + 2 * (mid + i) + part] = 1.0
                if i > 0:
                    table[(2 * part + 1) * hp + i, first + 2 * (mid - i) + part] = 1.0
        tables.append(table)
    return np.stack(tables).astype(ml_dtypes.bfloat16)


def split(x):
    hi = x.astype(BF16)
    lo = (x - hi.astype(F32)).astype(BF16)
    return hi, lo


def dot(a, b):
    return jnp.dot(a, b, preferred_element_type=F32)


def stream(x, table_ref):
    hi, lo = split(x)
    return dot(jnp.concatenate([hi, hi, lo], axis=1), table_ref[...])


def table_dot(table_ref, x):
    hi, lo = split(x)
    return dot(table_ref[...], jnp.concatenate([hi, lo, hi], axis=0))


def quarters(x, hp, fl):
    return x[:hp, :fl], x[:hp, fl:], x[hp:, :fl], x[hp:, fl:]


def block(a, b, c, d):
    top = jnp.concatenate([a, b], axis=1)
    low = jnp.concatenate([c, d], axis=1)
    return jnp.concatenate([top, low], axis=0)


def kernel(
    axis,
    n,
    chunk,
    params_ref,
    target_ref,
    weight_ref,
    kernels_ref,
    scale_ref,
    ids_ref,
    links_ref,
    rows_ref,
    freqs_ref,
    own_ref,
    side_ref,
    field_ref,
    adjoint_ref,
    middle_ref,
    outer_ref,
    fold_ref,
    out_ref,
    resist_ref,
    k_ref,
    h_ref,
    e_ref,
    t_ref,
    send_ref,
    recv_ref,
    send_sems,
    recv_sems,
    load_sem,
):
    me = lax.axis_index(axis)
    slots, rows, cols = params_ref.shape
    count, bands = h_ref.shape[0], k_ref.shape[1]
    hp, fl = h_ref.shape[1] // 2, h_ref.shape[2] // 2
    group = group_of(bands)
    unit = 1.0 / (rows * cols)
    step_size = STEP_SCALE * math.sqrt(rows * cols)
    has_left, has_right = me > 0, me < n - 1

    load = pltpu.make_async_copy(kernels_ref, k_ref, load_sem)
    load.start()
    barrier = pltpu.get_barrier_semaphore()

    @pl.when(has_left)
    def _():
        pl.semaphore_signal(
            barrier, inc=1, device_id={axis: me - 1}, device_id_type=pl.DeviceIdType.MESH
        )

    @pl.when(has_right)
    def _():
        pl.semaphore_signal(
            barrier, inc=1, device_id={axis: me + 1}, device_id_type=pl.DeviceIdType.MESH
        )

    peers = jnp.where(has_left, 1, 0) + jnp.where(has_right, 1, 0)
    pl.semaphore_wait(barrier, peers)

    @pl.when(jnp.logical_not(has_left))
    def _():
        for e in range(2 * ITERS):
            recv_ref[e, 0] = jnp.zeros((rows, cols), F32)

    @pl.when(jnp.logical_not(has_right))
    def _():
        for e in range(2 * ITERS):
            recv_ref[e, 1] = jnp.zeros((rows, cols), F32)

    def move(e, side):
        return pltpu.make_async_remote_copy(
            src_ref=send_ref.at[e, side],
            dst_ref=recv_ref.at[e, side],
            send_sem=send_sems.at[e, side],
            recv_sem=recv_sems.at[e, side],
            device_id={axis: me + 1 if side == 0 else me - 1},
            device_id_type=pl.DeviceIdType.MESH,
        )

    def start(e):
        @pl.when(has_right)
        def _():
            move(e, 0).start()

        @pl.when(has_left)
        def _():
            move(e, 1).start()

    def arrive(e):
        @pl.when(has_left)
        def _():
            move(e, 0).wait_recv()

        @pl.when(has_right)
        def _():
            move(e, 1).wait_recv()

    live = [ids_ref[s] >= 0 for s in range(slots)]
    left_on = [jnp.where(links_ref[s, 0] == 1, 1.0, 0.0) for s in range(slots)]
    right_on = [jnp.where(links_ref[s, 1] == 1, 1.0, 0.0) for s in range(slots)]

    def last_live(values):
        last = values[0]
        for s in range(1, slots):
            last = jnp.where(live[s], values[s], last)
        return last

    def neighbours(to_right, to_left, e):
        befores, afters = [], []
        for s in range(slots):
            before = recv_ref[e, 0] if s == 0 else to_right[s - 1]
            after = recv_ref[e, 1]
            if s + 1 < slots:
                after = jnp.where(live[s + 1], to_left[s + 1], after)
            befores.append(before * left_on[s])
            afters.append(after * right_on[s])
        return befores, afters

    for it in range(ITERS):
        source = params_ref if it == 0 else out_ref
        transmit = [jnp.tanh(source[s]) for s in range(slots)]
        for s in range(slots):
            t_ref[s] = transmit[s]
        send_ref[2 * it, 0] = last_live(transmit)
        send_ref[2 * it, 1] = transmit[0]
        start(2 * it)

        if it == 0:

            load.wait()

            def prepare(c, carry):
                span = group * 2 * bands
                base = pl.multiple_of(c * span, 8)
                for j in range(group):
                    begin, size = window_of(bands, j)
                    k = c * group + j
                    piece = k_ref[pl.ds(base + begin, size), :]
                    hi, lo = split(piece)
                    last = (piece - hi.astype(F32) - lo.astype(F32)).astype(BF16)
                    fold = fold_ref[j]
                    folded = dot(fold, hi) + dot(fold, lo) + dot(fold, last)
                    folded = folded * jnp.sqrt(jnp.full(folded.shape, scale_ref[k], F32))
                    h_ref[k] = jnp.zeros((2 * hp, 2 * fl), F32)
                    h_ref[k, :, :bands] = folded[: 2 * hp]
                    h_ref[k, :, fl : fl + bands] = folded[2 * hp :]
                return carry

            lax.fori_loop(0, count // group, prepare, 0)

        parts = stream(jnp.concatenate(transmit, axis=0), own_ref)
        arrive(2 * it)
        transmit = [t_ref[s] for s in range(slots)]
        befores, afters = neighbours(transmit, transmit, 2 * it)
        sides = [jnp.concatenate([befores[s], afters[s]], axis=1) for s in range(slots)]
        parts = parts + stream(jnp.concatenate(sides, axis=0), side_ref)
        spectra = []
        for s in range(slots):
            folded = table_dot(freqs_ref, parts[s * rows : (s + 1) * rows]) * unit
            ar, ai, br, bi = quarters(folded, hp, fl)
            spectra.append((ar + bi, ai - br, ar - bi, ai + br))

        def forward(c, intensities):
            out = []
            for s in range(slots):
                pr, pi, mr, mi = spectra[s]
                mids = []
                for j in range(chunk):
                    k = c * chunk + j
                    hpr, hpi, hmr, hmi = quarters(h_ref[k], hp, fl)
                    upr = hpr * pr - hpi * pi
                    upi = hpr * pi + hpi * pr
                    dnr = hmr * mr - hmi * mi
                    dni = hmr * mi + hmi * mr
                    mids.append(
                        table_dot(rows_ref, block(upr + dnr, upi + dni, dni - upi, upr - dnr))
                    )
                fields = stream(jnp.concatenate(mids, axis=0), field_ref)
                e_ref[s, c] = fields
                total = intensities[s]
                for j in range(chunk):
                    er = fields[j * rows : (j + 1) * rows, :cols]
                    ei = fields[j * rows : (j + 1) * rows, cols:]
                    total = total + er * er + ei * ei
                out.append(total)
            return tuple(out)

        zero = jnp.zeros((rows, cols), F32)
        intensities = lax.fori_loop(0, count // chunk, forward, (zero,) * slots)

        slopes = []
        for s in range(slots):
            now = jax.nn.sigmoid(RESIST_SLOPE * (intensities[s] - THRESHOLD))
            if it == ITERS - 1:
                resist_ref[s] = jnp.where(live[s], now, 0.0)
            slope = 2.0 * weight_ref[s] * (now - target_ref[s]) * RESIST_SLOPE * now * (1.0 - now)
            slopes.append(jnp.concatenate([slope, slope], axis=1))

        def backward(c, sums):
            out = []
            for s in range(slots):
                fields = e_ref[s, c]
                back = jnp.concatenate(
                    [fields[j * rows : (j + 1) * rows] * slopes[s] for j in range(chunk)], axis=0
                )
                columns = stream(back, adjoint_ref)
                spr, spi, smr, smi = sums[s]
                for j in range(chunk):
                    k = c * chunk + j
                    freq = table_dot(freqs_ref, columns[j * rows : (j + 1) * rows])
                    ar, ai, br, bi = quarters(freq, hp, fl)
                    hpr, hpi, hmr, hmi = quarters(h_ref[k], hp, fl)
                    gpr, gpi, gmr, gmi = ar - bi, ai + br, ar + bi, ai - br
                    spr = spr + hpr * gpr - hpi * gpi
                    spi = spi + hpr * gpi + hpi * gpr
                    smr = smr + hmr * gmr - hmi * gmi
                    smi = smi + hmr * gmi + hmi * gmr
                out.append((spr, spi, smr, smi))
            return tuple(out)

        none = jnp.zeros((hp, fl), F32)
        sums = lax.fori_loop(0, count // chunk, backward, ((none,) * 4,) * slots)

        uppers = []
        for s in range(slots):
            spr, spi, smr, smi = sums[s]
            uppers.append(
                table_dot(rows_ref, block(spr + smr, spi + smi, spi - smi, smr - spr))
            )
        upper = jnp.concatenate(uppers, axis=0)
        outer = stream(upper, outer_ref) * (2.0 * unit)
        to_left = [outer[s * rows : (s + 1) * rows, :cols] for s in range(slots)]
        to_right = [outer[s * rows : (s + 1) * rows, cols:] for s in range(slots)]
        send_ref[2 * it + 1, 0] = last_live(to_right)
        send_ref[2 * it + 1, 1] = to_left[0]
        start(2 * it + 1)
        inner = stream(upper, middle_ref) * (2.0 * unit)
        middle = [inner[s * rows : (s + 1) * rows] for s in range(slots)]
        arrive(2 * it + 1)
        befores, afters = neighbours(to_right, to_left, 2 * it + 1)
        for s in range(slots):
            gradient = middle[s] + befores[s] + afters[s]
            old = source[s]
            t = t_ref[s]
            new = old - step_size * gradient * (1.0 - t * t)
            out_ref[s] = jnp.where(live[s], new, old)

    for e in range(2 * ITERS):

        @pl.when(has_right)
        def _():
            move(e, 0).wait_send()

        @pl.when(has_left)
        def _():
            move(e, 1).wait_send()


def local(n, mask_params, target, weight, kernels, kernel_weight, tile_ids, tile_links):
    slots, rows, cols = mask_params.shape
    count, _, bands, _ = kernels.shape
    hp, fl = round_up((bands - 1) // 2 + 1, 8), round_up(bands, 128)
    chunk = next(c for c in (8, 4, 3, 2, 1) if count % c == 0)
    flat = kernels.transpose(0, 2, 1, 3).reshape(count * bands * 2, bands)
    tables = make_tables(rows, cols, bands)
    vmem = pl.BlockSpec(memory_space=pltpu.VMEM)
    smem = pl.BlockSpec(memory_space=pltpu.SMEM)
    shape = jax.ShapeDtypeStruct((slots, rows, cols), F32)
    return pl.pallas_call(
        functools.partial(kernel, "tile", n, chunk),
        out_shape=(shape, shape),
        in_specs=[vmem] * 3 + [pl.BlockSpec(memory_space=pl.ANY)] + [smem] * 3 + [vmem] * len(tables),
        out_specs=(vmem, vmem),
        scratch_shapes=[
            pltpu.VMEM(flat.shape, F32),
            pltpu.VMEM((count, 2 * hp, 2 * fl), F32),
            pltpu.VMEM((slots, count // chunk, chunk * rows, 2 * cols), F32),
            pltpu.VMEM((slots, rows, cols), F32),
            pltpu.VMEM((2 * ITERS, 2, rows, cols), F32),
            pltpu.VMEM((2 * ITERS, 2, rows, cols), F32),
            pltpu.SemaphoreType.DMA((2 * ITERS, 2)),
            pltpu.SemaphoreType.DMA((2 * ITERS, 2)),
            pltpu.SemaphoreType.DMA,
        ],
        compiler_params=pltpu.CompilerParams(
            collective_id=0, has_side_effects=True, vmem_limit_bytes=48 * 1024 * 1024
        ),
    )(
        mask_params,
        target,
        weight,
        flat,
        kernel_weight,
        tile_ids,
        tile_links,
        *[jnp.asarray(t) for t in tables],
    )


def solution(mesh):
    both = ("grp", "tile")
    return jax.shard_map(
        functools.partial(local, mesh.shape["tile"]),
        mesh=mesh,
        in_specs=(P(both, None, None),) * 3 + (P(), P(), P(both), P(both, None)),
        out_specs=(P(both, None, None),) * 2,
        check_vma=False,
    )
```

```python
import functools
import math

import jax
import jax.numpy as jnp
import ml_dtypes
import numpy as np
from jax import lax
from jax.experimental import pallas as pl
from jax.experimental.pallas import tpu as pltpu
from jax.sharding import PartitionSpec as P

ITERS = 2
RESIST_SLOPE = 4.0
THRESHOLD = 0.9
STEP_SCALE = 0.04
F32 = jnp.float32
BF16 = jnp.bfloat16


def round_up(size, step):
    return (size + step - 1) // step * step


def phases(length, period, bands):
    f = np.arange(bands, dtype=np.int64) - (bands - 1) // 2
    turns = (np.arange(length, dtype=np.int64)[:, None] * f[None, :]) % period
    angles = turns.astype(np.float64) * (2.0 * math.pi / period)
    return np.cos(angles), np.sin(angles)


def padded(table, rows, cols):
    return np.pad(table, ((0, rows - table.shape[0]), (0, cols - table.shape[1])))


def halves(table):
    table = table.astype(np.float32)
    hi = table.astype(ml_dtypes.bfloat16)
    lo = (table - hi.astype(np.float32)).astype(ml_dtypes.bfloat16)
    return hi, lo


def left_table(table):
    hi, lo = halves(table)
    return np.concatenate([hi, hi, lo], axis=1)


def right_table(table):
    hi, lo = halves(table)
    return np.concatenate([hi, lo, hi], axis=0)


def make_tables(rows, cols, bands):
    mid = (bands - 1) // 2
    hp, fl = round_up(mid + 1, 8), round_up(bands, 128)
    row_cos, row_sin = phases(rows, 2 * rows, bands)
    dom_cos, dom_sin = phases(3 * cols, 3 * cols, bands)
    own = slice(cols, 2 * cols)
    sides = np.r_[0:cols, 2 * cols : 3 * cols]
    up_cos, up_sin = padded(row_cos[:, mid:], rows, hp), padded(row_sin[:, mid:], rows, hp)
    to_rows = np.concatenate([up_cos, up_sin], axis=1)
    oc, os = padded(dom_cos[own].T, fl, cols), padded(dom_sin[own].T, fl, cols)
    field = np.block([[oc, os], [-os, oc]])
    adjoint = np.block([[oc.T, os.T], [os.T, -oc.T]])
    dc, ds = padded(dom_cos, 3 * cols, fl), padded(dom_sin, 3 * cols, fl)
    spectrum = np.concatenate([dc, -ds], axis=1)
    gradient = np.concatenate([dc.T, ds.T], axis=0)
    return (
        left_table(to_rows),
        left_table(to_rows.T),
        right_table(spectrum[own]),
        right_table(spectrum[sides]),
        right_table(field),
        right_table(adjoint),
        right_table(gradient[:, own]),
        right_table(gradient[:, sides]),
        fold_table(bands),
    )


def group_of(bands):
    return 8 // math.gcd(2 * bands, 8)


def window_of(bands, j):
    size = round_up(2 * bands + 6, 16)
    begin = min(j * 2 * bands // 8 * 8, group_of(bands) * 2 * bands - size)
    return begin, size


def fold_table(bands):
    mid = (bands - 1) // 2
    hp = round_up(mid + 1, 8)
    tables = []
    for j in range(group_of(bands)):
        begin, size = window_of(bands, j)
        table = np.zeros((4 * hp, size), np.float32)
        first = j * 2 * bands - begin
        for part in range(2):
            for i in range(mid + 1):
                table[2 * part * hp + i, first + 2 * (mid + i) + part] = 1.0
                if i > 0:
                    table[(2 * part + 1) * hp + i, first + 2 * (mid - i) + part] = 1.0
        tables.append(table)
    return np.stack(tables).astype(ml_dtypes.bfloat16)


def split(x):
    hi = x.astype(BF16)
    lo = (x - hi.astype(F32)).astype(BF16)
    return hi, lo


def dot(a, b):
    return jnp.dot(a, b, preferred_element_type=F32)


def stream(x, table_ref):
    hi, lo = split(x)
    return dot(jnp.concatenate([hi, hi, lo], axis=1), table_ref[...])


def table_dot(table_ref, x):
    hi, lo = split(x)
    return dot(table_ref[...], jnp.concatenate([hi, lo, hi], axis=0))


def quarters(x, hp, fl):
    return x[:hp, :fl], x[:hp, fl:], x[hp:, :fl], x[hp:, fl:]


def block(a, b, c, d):
    top = jnp.concatenate([a, b], axis=1)
    low = jnp.concatenate([c, d], axis=1)
    return jnp.concatenate([top, low], axis=0)


def kernel(
    axis,
    n,
    chunk,
    params_ref,
    target_ref,
    weight_ref,
    k_ref,
    scale_ref,
    ids_ref,
    links_ref,
    rows_ref,
    freqs_ref,
    own_ref,
    side_ref,
    field_ref,
    adjoint_ref,
    middle_ref,
    outer_ref,
    fold_ref,
    out_ref,
    resist_ref,
    h_ref,
    e_ref,
    t_ref,
    send_ref,
    recv_ref,
    send_sems,
    recv_sems,
):
    me = lax.axis_index(axis)
    slots, rows, cols = params_ref.shape
    count, bands = h_ref.shape[0], k_ref.shape[1]
    hp, fl = h_ref.shape[1] // 2, h_ref.shape[2] // 2
    group = group_of(bands)
    unit = 1.0 / (rows * cols)
    step_size = STEP_SCALE * math.sqrt(rows * cols)
    has_left, has_right = me > 0, me < n - 1

    barrier = pltpu.get_barrier_semaphore()

    @pl.when(has_left)
    def _():
        pl.semaphore_signal(
            barrier, inc=1, device_id={axis: me - 1}, device_id_type=pl.DeviceIdType.MESH
        )

    @pl.when(has_right)
    def _():
        pl.semaphore_signal(
            barrier, inc=1, device_id={axis: me + 1}, device_id_type=pl.DeviceIdType.MESH
        )

    peers = jnp.where(has_left, 1, 0) + jnp.where(has_right, 1, 0)
    pl.semaphore_wait(barrier, peers)

    @pl.when(jnp.logical_not(has_left))
    def _():
        for e in range(2 * ITERS):
            recv_ref[e, 0] = jnp.zeros((rows, cols), F32)

    @pl.when(jnp.logical_not(has_right))
    def _():
        for e in range(2 * ITERS):
            recv_ref[e, 1] = jnp.zeros((rows, cols), F32)

    def move(e, side):
        return pltpu.make_async_remote_copy(
            src_ref=send_ref.at[e, side],
            dst_ref=recv_ref.at[e, side],
            send_sem=send_sems.at[e, side],
            recv_sem=recv_sems.at[e, side],
            device_id={axis: me + 1 if side == 0 else me - 1},
            device_id_type=pl.DeviceIdType.MESH,
        )

    def start(e):
        @pl.when(has_right)
        def _():
            move(e, 0).start()

        @pl.when(has_left)
        def _():
            move(e, 1).start()

    def arrive(e):
        @pl.when(has_left)
        def _():
            move(e, 0).wait_recv()

        @pl.when(has_right)
        def _():
            move(e, 1).wait_recv()

    live = [ids_ref[s] >= 0 for s in range(slots)]
    left_on = [jnp.where(links_ref[s, 0] == 1, 1.0, 0.0) for s in range(slots)]
    right_on = [jnp.where(links_ref[s, 1] == 1, 1.0, 0.0) for s in range(slots)]

    def last_live(values):
        last = values[0]
        for s in range(1, slots):
            last = jnp.where(live[s], values[s], last)
        return last

    def neighbours(to_right, to_left, e):
        befores, afters = [], []
        for s in range(slots):
            before = recv_ref[e, 0] if s == 0 else to_right[s - 1]
            after = recv_ref[e, 1]
            if s + 1 < slots:
                after = jnp.where(live[s + 1], to_left[s + 1], after)
            befores.append(before * left_on[s])
            afters.append(after * right_on[s])
        return befores, afters

    for it in range(ITERS):
        source = params_ref if it == 0 else out_ref
        transmit = [jnp.tanh(source[s]) for s in range(slots)]
        for s in range(slots):
            t_ref[s] = transmit[s]
        send_ref[2 * it, 0] = last_live(transmit)
        send_ref[2 * it, 1] = transmit[0]
        start(2 * it)

        if it == 0:

            def prepare(c, carry):
                span = group * 2 * bands
                base = pl.multiple_of(c * span, 8)
                for j in range(group):
                    begin, size = window_of(bands, j)
                    k = c * group + j
                    piece = k_ref[pl.ds(base + begin, size), :]
                    hi, lo = split(piece)
                    last = (piece - hi.astype(F32) - lo.astype(F32)).astype(BF16)
                    fold = fold_ref[j]
                    folded = dot(fold, hi) + dot(fold, lo) + dot(fold, last)
                    folded = folded * jnp.sqrt(jnp.full(folded.shape, scale_ref[k], F32))
                    h_ref[k] = jnp.zeros((2 * hp, 2 * fl), F32)
                    h_ref[k, :, :bands] = folded[: 2 * hp]
                    h_ref[k, :, fl : fl + bands] = folded[2 * hp :]
                return carry

            lax.fori_loop(0, count // group, prepare, 0)

        parts = stream(jnp.concatenate(transmit, axis=0), own_ref)
        arrive(2 * it)
        transmit = [t_ref[s] for s in range(slots)]
        befores, afters = neighbours(transmit, transmit, 2 * it)
        sides = [jnp.concatenate([befores[s], afters[s]], axis=1) for s in range(slots)]
        parts = parts + stream(jnp.concatenate(sides, axis=0), side_ref)
        spectra = []
        for s in range(slots):
            folded = table_dot(freqs_ref, parts[s * rows : (s + 1) * rows]) * unit
            ar, ai, br, bi = quarters(folded, hp, fl)
            spectra.append((ar + bi, ai - br, ar - bi, ai + br))

        def forward(c, intensities):
            out = []
            for s in range(slots):
                pr, pi, mr, mi = spectra[s]
                mids = []
                for j in range(chunk):
                    k = c * chunk + j
                    hpr, hpi, hmr, hmi = quarters(h_ref[k], hp, fl)
                    upr = hpr * pr - hpi * pi
                    upi = hpr * pi + hpi * pr
                    dnr = hmr * mr - hmi * mi
                    dni = hmr * mi + hmi * mr
                    mids.append(
                        table_dot(rows_ref, block(upr + dnr, upi + dni, dni - upi, upr - dnr))
                    )
                fields = stream(jnp.concatenate(mids, axis=0), field_ref)
                e_ref[s, c] = fields
                total = intensities[s]
                for j in range(chunk):
                    er = fields[j * rows : (j + 1) * rows, :cols]
                    ei = fields[j * rows : (j + 1) * rows, cols:]
                    total = total + er * er + ei * ei
                out.append(total)
            return tuple(out)

        zero = jnp.zeros((rows, cols), F32)
        intensities = lax.fori_loop(0, count // chunk, forward, (zero,) * slots)

        slopes = []
        for s in range(slots):
            now = jax.nn.sigmoid(RESIST_SLOPE * (intensities[s] - THRESHOLD))
            if it == ITERS - 1:
                resist_ref[s] = jnp.where(live[s], now, 0.0)
            slope = 2.0 * weight_ref[s] * (now - target_ref[s]) * RESIST_SLOPE * now * (1.0 - now)
            slopes.append(jnp.concatenate([slope, slope], axis=1))

        def backward(c, sums):
            out = []
            for s in range(slots):
                fields = e_ref[s, c]
                back = jnp.concatenate(
                    [fields[j * rows : (j + 1) * rows] * slopes[s] for j in range(chunk)], axis=0
                )
                columns = stream(back, adjoint_ref)
                spr, spi, smr, smi = sums[s]
                for j in range(chunk):
                    k = c * chunk + j
                    freq = table_dot(freqs_ref, columns[j * rows : (j + 1) * rows])
                    ar, ai, br, bi = quarters(freq, hp, fl)
                    hpr, hpi, hmr, hmi = quarters(h_ref[k], hp, fl)
                    gpr, gpi, gmr, gmi = ar - bi, ai + br, ar + bi, ai - br
                    spr = spr + hpr * gpr - hpi * gpi
                    spi = spi + hpr * gpi + hpi * gpr
                    smr = smr + hmr * gmr - hmi * gmi
                    smi = smi + hmr * gmi + hmi * gmr
                out.append((spr, spi, smr, smi))
            return tuple(out)

        none = jnp.zeros((hp, fl), F32)
        sums = lax.fori_loop(0, count // chunk, backward, ((none,) * 4,) * slots)

        uppers = []
        for s in range(slots):
            spr, spi, smr, smi = sums[s]
            uppers.append(
                table_dot(rows_ref, block(spr + smr, spi + smi, spi - smi, smr - spr))
            )
        upper = jnp.concatenate(uppers, axis=0)
        outer = stream(upper, outer_ref) * (2.0 * unit)
        to_left = [outer[s * rows : (s + 1) * rows, :cols] for s in range(slots)]
        to_right = [outer[s * rows : (s + 1) * rows, cols:] for s in range(slots)]
        send_ref[2 * it + 1, 0] = last_live(to_right)
        send_ref[2 * it + 1, 1] = to_left[0]
        start(2 * it + 1)
        inner = stream(upper, middle_ref) * (2.0 * unit)
        middle = [inner[s * rows : (s + 1) * rows] for s in range(slots)]
        arrive(2 * it + 1)
        befores, afters = neighbours(to_right, to_left, 2 * it + 1)
        for s in range(slots):
            gradient = middle[s] + befores[s] + afters[s]
            old = source[s]
            t = t_ref[s]
            new = old - step_size * gradient * (1.0 - t * t)
            out_ref[s] = jnp.where(live[s], new, old)

    for e in range(2 * ITERS):

        @pl.when(has_right)
        def _():
            move(e, 0).wait_send()

        @pl.when(has_left)
        def _():
            move(e, 1).wait_send()


def staged(axis, n, chunk, held, inputs, *refs):
    fixed, rest = list(refs[:inputs]), refs[inputs:]
    buffers, sems = rest[-1 - len(held) : -1], rest[-1]
    loads = [
        pltpu.make_async_copy(fixed[i], buffer, sems.at[j])
        for j, (i, buffer) in enumerate(zip(held, buffers))
    ]
    for load in loads:
        load.start()
    for load in loads:
        load.wait()
    for i, buffer in zip(held, buffers):
        fixed[i] = buffer
    kernel(axis, n, chunk, *fixed, *rest[: -1 - len(held)])


def local(n, mask_params, target, weight, kernels, kernel_weight, tile_ids, tile_links):
    slots, rows, cols = mask_params.shape
    count, _, bands, _ = kernels.shape
    hp, fl = round_up((bands - 1) // 2 + 1, 8), round_up(bands, 128)
    chunk = next(c for c in (12, 8, 4, 3, 2, 1) if count % c == 0)
    flat = kernels.transpose(0, 2, 1, 3).reshape(count * bands * 2, bands)
    tables = make_tables(rows, cols, bands)
    vmem = pl.BlockSpec(memory_space=pltpu.VMEM)
    smem = pl.BlockSpec(memory_space=pltpu.SMEM)
    shape = jax.ShapeDtypeStruct((slots, rows, cols), F32)
    anywhere = pl.BlockSpec(memory_space=pl.ANY)
    operands = [mask_params, target, weight, flat, kernel_weight, tile_ids, tile_links]
    operands += [jnp.asarray(t) for t in tables]
    held = [i for i in range(len(operands)) if i not in (4, 5, 6)]
    return pl.pallas_call(
        functools.partial(staged, "tile", n, chunk, held, len(operands)),
        out_shape=(shape, shape),
        in_specs=[anywhere] * 4 + [smem] * 3 + [anywhere] * len(tables),
        out_specs=(vmem, vmem),
        scratch_shapes=[
            pltpu.VMEM((count, 2 * hp, 2 * fl), F32),
            pltpu.VMEM((slots, count // chunk, chunk * rows, 2 * cols), F32),
            pltpu.VMEM((slots, rows, cols), F32),
            pltpu.VMEM((2 * ITERS, 2, rows, cols), F32),
            pltpu.VMEM((2 * ITERS, 2, rows, cols), F32),
            pltpu.SemaphoreType.DMA((2 * ITERS, 2)),
            pltpu.SemaphoreType.DMA((2 * ITERS, 2)),
            *[pltpu.VMEM(operands[i].shape, operands[i].dtype) for i in held],
            pltpu.SemaphoreType.DMA((len(held),)),
        ],
        compiler_params=pltpu.CompilerParams(
            collective_id=0, has_side_effects=True, vmem_limit_bytes=63 * 1024 * 1024
        ),
    )(*operands)


def solution(mesh):
    both = ("grp", "tile")
    return jax.shard_map(
        functools.partial(local, mesh.shape["tile"]),
        mesh=mesh,
        in_specs=(P(both, None, None),) * 3 + (P(), P(), P(both), P(both, None)),
        out_specs=(P(both, None, None),) * 2,
        check_vma=False,
    )
```
